32 devices in a mesh: row: 8 (over z, core), col: 4 (over y, x).
Axes of the slice: x: 2, y: 2, z: 4, core: 2. Of those that a mesh axis runs over, the one named last changes fastest.
Arguments:
- left_prop: float32 [8, 8, 2, 512, 512], P('row', None, None, 'col'), may hold values from -0.1875 to 0.1875
- vertex: float32 [8, 2, 512, 512], P(None, None, ('row', 'col')), may hold values from -5 to 5
- right_prop: float32 [8, 8, 2, 512, 512], P(None, 'col', None, None, 'row'), may hold values from -0.1875 to 0.1875
- insertions: int32 [3], replicated, may hold values from 0 to 7
- window_start: int32 [2], replicated, may hold values from 0 to 255
Outputs:
- correlator: float32 [8, 8, 2, 512, 512], P('row', 'col')
The draws below stay inside these ranges and needn't reach their ends.
Inputs may be any that keep to these rules, and one draw needn't show every extreme that they name: `insertions`: repeats may occur.
All inputs are finite; a program needn't handle non-finite values.
Results may differ from the reference program's by a relative error of at most 0.0001.
Values sent between devices are 32-bit elements; how exact they have to be, the bound alone decides.
A program may use at most 128 MiB of HBM per device.

```python
import jax
import jax.numpy as jnp
from jax import lax

NS = 8
LT = 256
INSERTS = 3
M = 512
T_SRC = 8
T_SNK = 8


def shard_levels(own_key, extent, shards, smallest, largest):
    def one(dim, blocks):
        steps = jax.random.uniform(jax.random.fold_in(jax.random.fold_in(own_key, 6), dim), (blocks,), jnp.float32, smallest / len(shards), largest / len(shards))
        return jnp.repeat(jnp.exp(steps), extent[dim] // blocks).reshape((-1,) + (1,) * (len(extent) - dim - 1))

    gain = one(*shards[0])
    for cut in shards[1:]:
        gain = gain * one(*cut)
    return gain


def bell_draw(rng, dims, deviation, bound, shards=(), kind=jnp.bfloat16):
    entries = jax.random.normal(rng, dims, jnp.float32) * deviation
    if len(shards) > 0:
        entries = shard_levels(rng, dims, shards, -0.22, 0.18) * entries
    return jnp.clip(entries, min=-bound, max=bound).astype(kind)


def setup_inputs(seed: int = 0) -> dict:
    key_of = jax.random.split(jax.random.key(seed), 6)
    return {
        "left_prop": bell_draw(key_of[0], (T_SRC, NS, 2, M, M), (2 * M) ** -0.5, 0.1875, ((0, 8), (3, 4)), jnp.float32),
        "vertex": bell_draw(key_of[1], (NS, 2, M, M), 0.7071, 5.0, ((2, 32),), jnp.float32),
        "right_prop": bell_draw(key_of[2], (NS, T_SNK, 2, M, M), (2 * M) ** -0.5, 0.1875, ((1, 4), (4, 8)), jnp.float32),
        "insertions": jax.random.randint(key_of[3], (INSERTS,), 0, NS).astype(jnp.int32),
        "window_start": jax.random.randint(key_of[4], (2,), 0, LT).astype(jnp.int32),
    }


def complex_product(first, second):
    highest = lax.Precision.HIGHEST
    first_re, first_im = first[..., 0, :, :], first[..., 1, :, :]
    second_re, second_im = second[..., 0, :, :], second[..., 1, :, :]
    real_part = jnp.matmul(first_re, second_re, precision=highest) - jnp.matmul(first_im, second_im, precision=highest)
    imag_part = jnp.matmul(first_re, second_im, precision=highest) + jnp.matmul(first_im, second_re, precision=highest)
    return jnp.stack([real_part, imag_part], axis=-3)


def boundary_signs(insertions, window_start, source_slots, sink_slots):
    slice_times = insertions * (LT // NS)
    source_times = (window_start[0] + source_slots) % LT
    sink_times = (window_start[1] + sink_slots) % LT
    left_sign = jnp.where(slice_times[None, :] < source_times[:, None], -1.0, 1.0).astype(jnp.float32)
    right_sign = jnp.where(sink_times[None, :] < slice_times[:, None], -1.0, 1.0).astype(jnp.float32)
    return left_sign, right_sign


def reference(left_prop, vertex, right_prop, insertions, window_start):
    source_slots = jnp.arange(T_SRC, dtype=jnp.int32)
    sink_slots = jnp.arange(T_SNK, dtype=jnp.int32)
    left_sign, right_sign = boundary_signs(insertions, window_start, source_slots, sink_slots)
    chosen_left = jnp.take(left_prop, insertions, axis=1) * left_sign[:, :, None, None, None]
    vertex_full = jnp.take(vertex, insertions, axis=0)
    chosen_right = jnp.take(right_prop, insertions, axis=0) * right_sign[:, :, None, None, None]

    def one_source(left_blocks):
        through = complex_product(left_blocks, vertex_full)
        summed = jnp.zeros((T_SNK, 2, M, M), jnp.float32)
        for which in range(INSERTS):
            summed = summed + complex_product(through[which][None], chosen_right[which])
        return summed

    return lax.map(one_source, chosen_left)
```

```python
import functools

import jax
import jax.numpy as jnp
from jax import lax
from jax.experimental import pallas as pl
from jax.experimental.pallas import tpu as pltpu
from jax.sharding import PartitionSpec as P

NS = 8
LT = 256
MESH = pl.DeviceIdType.MESH
F32 = jnp.float32
BF16 = jnp.bfloat16


def choose_kernel(ins, left_sign, right_sign, left_ref, vertex_ref, right_ref, l_ref, v_ref, r_ref):
    k = pl.program_id(0)
    l_ref[0] = left_ref[0, 0] * left_sign[k]
    v_ref[0] = vertex_ref[0]
    for u in range(right_ref.shape[1]):
        for part in range(2):
            r_ref[0, part, u] = right_ref[0, u, part] * right_sign[k, u]


def choose(left_prop, vertex, right_t, insertions, left_sign, right_sign):
    count = insertions.shape[0]
    _, _, _, lrows, m = left_prop.shape
    vrows = vertex.shape[2]
    sinks, cols = right_t.shape[1], right_t.shape[3]
    return pl.pallas_call(
        choose_kernel,
        grid_spec=pltpu.PrefetchScalarGridSpec(
            num_scalar_prefetch=3,
            grid=(count,),
            in_specs=[
                pl.BlockSpec((1, 1, 2, lrows, m), lambda k, i, *_: (0, i[k], 0, 0, 0)),
                pl.BlockSpec((1, 2, vrows, m), lambda k, i, *_: (i[k], 0, 0, 0)),
                pl.BlockSpec((1, sinks, 2, cols, m), lambda k, i, *_: (i[k], 0, 0, 0, 0)),
            ],
            out_specs=[
                pl.BlockSpec((1, 2, lrows, m), lambda k, *_: (k, 0, 0, 0)),
                pl.BlockSpec((1, 2, vrows, m), lambda k, *_: (k, 0, 0, 0)),
                pl.BlockSpec((1, 2, sinks, cols, m), lambda k, *_: (k, 0, 0, 0, 0)),
            ],
        ),
        out_shape=[
            jax.ShapeDtypeStruct((count, 2, lrows, m), F32),
            jax.ShapeDtypeStruct((count, 2, vrows, m), F32),
            jax.ShapeDtypeStruct((count, 2, sinks, cols, m), F32),
        ],
    )(insertions, left_sign, right_sign, left_prop, vertex, right_t)


def halves(x):
    high = x.astype(BF16)
    return high, (x - high.astype(F32)).astype(BF16)


def dot_nn(a, b):
    return lax.dot_general(a, b, (((1,), (0,)), ((), ())), preferred_element_type=F32)


def dot_nt(a, b):
    return lax.dot_general(a, b, (((1,), (1,)), ((), ())), preferred_element_type=F32)


def main_kernel(
    nz, l_ref, v_ref, r_ref, out_ref,
    v_all, r_all, lv_all, lv_high, lv_low, acc,
    v_send_z, v_send, v_recv, r_send, r_recv, lv_send, lv_recv,
):
    count, _, lrows, m = l_ref.shape
    vrows = v_ref.shape[2]
    sinks = out_ref.shape[1]
    rrows = r_ref.shape[1]
    half = rrows // 2
    cols = half // sinks
    ncol = 4
    row, c = lax.axis_index("row"), lax.axis_index("col")
    z, h = row // 2, lax.rem(row, 2)
    cx = c + 1 - 2 * lax.rem(c, 2)
    cy = lax.rem(c + 2, ncol)
    cd = lax.rem(cx + 2, ncol)
    sib = (2 * z + 1 - h, c)
    to_x, to_y = (row, cx), (row, cy)
    up, down = (row + 2, c), (row - 2, c)

    barrier = pltpu.get_barrier_semaphore()
    for dz in range(1, nz):
        pl.semaphore_signal(barrier, inc=1, device_id=(2 * lax.rem(z + dz, nz) + h, c), device_id_type=MESH)
    for dev in (sib, to_x, to_y):
        pl.semaphore_signal(barrier, inc=1, device_id=dev, device_id_type=MESH)
    pl.semaphore_wait(barrier, nz - 1 + 3)

    pending = []

    def send(src, dst, ssem, rsem, dev, when=None):
        def make():
            return pltpu.make_async_remote_copy(
                src_ref=src(), dst_ref=dst(), send_sem=ssem(), recv_sem=rsem(), device_id=dev, device_id_type=MESH
            )

        if when is None:
            make().start()
        else:
            pl.when(when)(lambda: make().start())
        pending.append((when, make))

    def arrived(dst, rsem):
        pltpu.make_async_remote_copy(
            src_ref=dst, dst_ref=dst, send_sem=v_send_z.at[0], recv_sem=rsem, device_id=sib, device_id_type=MESH
        ).wait_recv()

    def v_slot(zs, hs, cs):
        return v_all.at[:, :, pl.ds(pl.multiple_of(((2 * zs + hs) * ncol + cs) * vrows, vrows), vrows), :]

    def v_sem(zs, hs, cs):
        return v_recv.at[(2 * zs + hs) * ncol + cs]

    for dz in range(1, nz):
        send(
            lambda: v_ref, lambda: v_slot(z, h, c), lambda dz=dz: v_send_z.at[dz], lambda: v_sem(z, h, c),
            (2 * lax.rem(z + dz, nz) + h, c),
        )

    def v_pass(kind, j, mm, src, zs, cs, dev):
        send(src, lambda: v_slot(zs, h, cs), lambda: v_send.at[kind, j, mm], lambda: v_sem(zs, h, cs), dev)

    for mm in range(nz):
        zs = lax.rem(z + mm, nz)
        if mm == 0:
            src = lambda: v_ref
        else:
            src = lambda zs=zs: v_slot(zs, h, c)
            arrived(v_slot(zs, h, c), v_sem(zs, h, c))
        v_pass(0, 0, mm, src, zs, c, to_x)
        v_pass(1, 0, mm, src, zs, c, to_y)
        v_pass(2, 0, mm, src, zs, c, sib)
    v_all[:, :, pl.ds(pl.multiple_of((row * ncol + c) * vrows, vrows), vrows), :] = v_ref[...]

    def r_pass(kind, zs, k, src, dev, when=None):
        send(
            src, lambda: r_all.at[2 * zs + h, k], lambda: r_send.at[kind, zs, k], lambda: r_recv.at[2 * zs + h, k],
            dev, when,
        )

    has_up, has_down = z < nz - 1, z > 0
    for k in range(count):
        src = lambda k=k: r_ref.at[k]
        r_pass(0, z, k, src, up, has_up)
        r_pass(1, z, k, src, down, has_down)
    for k in range(count):
        r_pass(2, z, k, lambda k=k: r_ref.at[k], sib)
    r_all[row] = r_ref[...]

    hops = {}
    for d in range(1, nz):
        low_ok, high_ok = z - d >= 0, z + d < nz
        hops[d] = (
            (0, up, z - d, low_ok, jnp.logical_and(low_ok, has_up)),
            (1, down, z + d, high_ok, jnp.logical_and(high_ok, has_down)),
        )

    def r_step(d):
        for k in range(count):
            for kind, toward, zs, ok, onward in hops[d]:
                src = lambda zs=zs, k=k: r_all.at[2 * zs + h, k]

                @pl.when(ok)
                def _(zs=zs, k=k, src=src):
                    arrived(src(), r_recv.at[2 * zs + h, k])

                if d < nz - 1:
                    r_pass(kind, zs, k, src, toward, onward)
                r_pass(2, zs, k, src, sib, ok)

    for mm in range(nz):
        zs = lax.rem(z + mm, nz)
        arrived(v_slot(zs, h, cx), v_sem(zs, h, cx))
        src = lambda zs=zs: v_slot(zs, h, cx)
        if mm < nz // 2:
            v_pass(1, 1, mm, src, zs, cx, to_y)
        v_pass(2, 1, mm, src, zs, cx, sib)
        arrived(v_slot(zs, h, cy), v_sem(zs, h, cy))
        src = lambda zs=zs: v_slot(zs, h, cy)
        if mm >= nz // 2:
            v_pass(0, 1, mm, src, zs, cy, to_x)
        v_pass(2, 2, mm, src, zs, cy, sib)
    for mm in range(nz):
        zs = lax.rem(z + mm, nz)
        arrived(v_slot(zs, h, cd), v_sem(zs, h, cd))
        v_pass(2, 3, mm, lambda zs=zs: v_slot(zs, h, cd), zs, cd, sib)
    for mm in range(nz):
        zs = lax.rem(z + mm, nz)
        for cs in (c, cx, cy, cd):
            arrived(v_slot(zs, 1 - h, cs), v_sem(zs, 1 - h, cs))

    def lv_piece(cs, k, part):
        return lv_all.at[cs, k, part]

    def lv_pass(kind, fwd, k, part, cs, dev):
        send(
            lambda: lv_piece(cs, k, part), lambda: lv_piece(cs, k, part),
            lambda: lv_send.at[kind, fwd, k, part], lambda: lv_recv.at[cs, k, part], dev,
        )

    def split_lv(cs, k, part):
        high, low = halves(lv_all[cs, k, part])
        at = pl.ds(pl.multiple_of(part * m + cs * lrows, lrows), lrows)
        lv_high[k, at, :] = high
        lv_low[k, at, :] = low

    for k in range(count):
        xh, xl = halves(l_ref[k].reshape(2 * lrows, m))
        prods = []
        for part in range(2):
            vh, vl = halves(v_all[k, part])
            prods.append(dot_nn(xh, vh) + dot_nn(xl, vh) + dot_nn(xh, vl))
        lv_all[c, k, 0] = prods[0][:lrows] - prods[1][lrows:]
        lv_all[c, k, 1] = prods[1][:lrows] + prods[0][lrows:]
        for part in range(2):
            lv_pass(0, 0, k, part, c, to_x)
            lv_pass(1, 0, k, part, c, to_y)

    r_step(1)

    for k in range(count):
        for part in range(2):
            split_lv(c, k, part)
    for k in range(count):
        for part in range(2):
            arrived(lv_piece(cx, k, part), lv_recv.at[cx, k, part])
            if part == 0:
                lv_pass(1, 1, k, part, cx, to_y)
            arrived(lv_piece(cy, k, part), lv_recv.at[cy, k, part])
            if part == 1:
                lv_pass(0, 1, k, part, cy, to_x)
            split_lv(cx, k, part)
            split_lv(cy, k, part)
    for d in range(2, nz - 1):
        r_step(d)
    for k in range(count):
        for part in range(2):
            arrived(lv_piece(cd, k, part), lv_recv.at[cd, k, part])
            split_lv(cd, k, part)

    def chip(i, carry):
        d = (i + 1) // 2
        q = z + d * (1 - 2 * lax.rem(i, 2))
        if nz > 2:
            pl.when(i == 2 * (nz - 1) - 1)(lambda: r_step(nz - 1))

        @pl.when(jnp.logical_and(q >= 0, q < nz))
        def _():
            for k in range(count):
                arrived(r_all.at[2 * q + 1 - h, k], r_recv.at[2 * q + 1 - h, k])

            def one(j, carry):
                for k in range(count):
                    yh, yl = halves(r_all[2 * q + j, k])
                    for part in range(2):
                        at = pl.ds(part * m, m)
                        p = (
                            dot_nt(lv_high[k, at, :], yh)
                            + dot_nt(lv_low[k, at, :], yh)
                            + dot_nt(lv_high[k, at, :], yl)
                        )
                        if k == 0:
                            acc[j, at, :] = p
                        else:
                            acc[j, at, :] += p
                return carry

            lax.fori_loop(0, 2, one, 0)
            real, imag = [], []
            for j in range(2):
                real.append(acc[j, pl.ds(0, m), pl.ds(0, half)] - acc[j, pl.ds(m, m), pl.ds(half, half)])
                imag.append(acc[j, pl.ds(0, m), pl.ds(half, half)] + acc[j, pl.ds(m, m), pl.ds(0, half)])
            for u in range(sinks):
                cut = slice(u * cols, (u + 1) * cols)
                out_ref[q, u, 0] = jnp.concatenate([real[0][:, cut], real[1][:, cut]], axis=1)
                out_ref[q, u, 1] = jnp.concatenate([imag[0][:, cut], imag[1][:, cut]], axis=1)

        return carry

    lax.fori_loop(0, 2 * nz - 1, chip, 0)

    for when, make in pending:
        if when is None:
            make().wait_send()
        else:
            pl.when(when)(lambda make=make: make().wait_send())


def exchange_and_contract(nrow, ncol, chosen_left, chosen_vertex, chosen_right):
    count, _, lrows, m = chosen_left.shape
    vrows = chosen_vertex.shape[2]
    sinks, cols = chosen_right.shape[2], chosen_right.shape[3]
    rrows = 2 * sinks * cols
    nz = nrow // 2
    dma = pltpu.SemaphoreType.DMA
    vmem = pl.BlockSpec(memory_space=pltpu.VMEM)
    return pl.pallas_call(
        functools.partial(main_kernel, nz),
        out_shape=jax.ShapeDtypeStruct((nz, sinks, 2, m, 2 * cols), F32),
        in_specs=[vmem, vmem, vmem],
        out_specs=vmem,
        scratch_shapes=[
            pltpu.VMEM((count, 2, nrow * ncol * vrows, m), F32),
            pltpu.VMEM((nrow, count, rrows, m), F32),
            pltpu.VMEM((ncol, count, 2, lrows, m), F32),
            pltpu.VMEM((count, 2 * m, m), BF16),
            pltpu.VMEM((count, 2 * m, m), BF16),
            pltpu.VMEM((2, 2 * m, rrows), F32),
            dma((nz,)),
            dma((3, 4, nz)),
            dma((nrow * ncol,)),
            dma((3, nz, count)),
            dma((nrow, count)),
            dma((2, 2, count, 2)),
            dma((ncol, count, 2)),
        ],
        compiler_params=pltpu.CompilerParams(
            collective_id=0, has_side_effects=True, vmem_limit_bytes=58 * 1024 * 1024
        ),
    )(chosen_left, chosen_vertex, chosen_right.reshape(count, rrows, m))


def complex_product(first, second):
    highest = lax.Precision.HIGHEST
    first_re, first_im = first[..., 0, :, :], first[..., 1, :, :]
    second_re, second_im = second[..., 0, :, :], second[..., 1, :, :]
    real_part = jnp.matmul(first_re, second_re, precision=highest) - jnp.matmul(first_im, second_im, precision=highest)
    imag_part = jnp.matmul(first_re, second_im, precision=highest) + jnp.matmul(first_im, second_re, precision=highest)
    return jnp.stack([real_part, imag_part], axis=-3)


def pick(array, insertions, axis):
    parts = [lax.dynamic_index_in_dim(array, insertions[k], axis, keepdims=True) for k in range(insertions.shape[0])]
    return jnp.concatenate(parts, axis=axis)


def general(left_prop, vertex, right_prop, insertions, left_sign, right_sign):
    chosen_left = pick(left_prop, insertions, 1) * left_sign[:, :, None, None, None]
    chosen_right = pick(right_prop, insertions, 0) * right_sign[:, :, None, None, None]
    vertex_full = lax.all_gather(pick(vertex, insertions, 0), ("row", "col"), axis=2, tiled=True)
    through = complex_product(chosen_left, vertex_full[None])
    through = lax.all_gather(through, "col", axis=3, tiled=True)
    right_full = lax.all_gather(chosen_right, "row", axis=4, tiled=True)
    summed = complex_product(through[:, 0, None], right_full[0][None])
    for k in range(1, insertions.shape[0]):
        summed = summed + complex_product(through[:, k, None], right_full[k][None])
    return summed


def per_device(nrow, ncol, left_prop, vertex, right_prop, insertions, window_start):
    source_count = left_prop.shape[0]
    sink_count = right_prop.shape[1]
    source_slots = lax.axis_index("row") * source_count + jnp.arange(source_count, dtype=jnp.int32)
    sink_slots = lax.axis_index("col") * sink_count + jnp.arange(sink_count, dtype=jnp.int32)
    slice_times = insertions * (LT // NS)
    source_times = (window_start[0] + source_slots) % LT
    sink_times = (window_start[1] + sink_slots) % LT
    left_sign = jnp.where(slice_times[None, :] < source_times[:, None], -1.0, 1.0).astype(F32)
    right_sign = jnp.where(sink_times[None, :] < slice_times[:, None], -1.0, 1.0).astype(F32)
    lrows, m = left_prop.shape[3:]
    fits = (
        source_count == 1 and ncol == 4 and nrow % 2 == 0 and nrow >= 4 and vertex.shape[2] % 8 == 0
        and lrows % 16 == 0 and m % 128 == 0 and 2 * right_prop.shape[4] == 128
        and right_prop.shape[1] * right_prop.shape[4] == 128
    )
    if not fits:
        return general(left_prop, vertex, right_prop, insertions, left_sign, right_sign)
    chosen = choose(
        left_prop, vertex, jnp.swapaxes(right_prop, 3, 4), insertions, left_sign[0], right_sign
    )
    blocks = exchange_and_contract(nrow, ncol, *chosen)
    nz, sinks, _, _, width = blocks.shape
    return jnp.transpose(blocks, (1, 2, 3, 0, 4)).reshape(1, sinks, 2, m, nz * width)


def solution(mesh):
    return jax.shard_map(
        functools.partial(per_device, mesh.shape["row"], mesh.shape["col"]),
        mesh=mesh,
        in_specs=(
            P("row", None, None, "col", None),
            P(None, None, ("row", "col"), None),
            P(None, "col", None, None, "row"),
            P(),
            P(),
        ),
        out_specs=P("row", "col", None, None, None),
        check_vma=False,
    )
```

```python
import functools

import jax
import jax.numpy as jnp
from jax import lax
from jax.experimental import pallas as pl
from jax.experimental.pallas import tpu as pltpu
from jax.sharding import PartitionSpec as P

NS = 8
LT = 256
MESH = pl.DeviceIdType.MESH
F32 = jnp.float32
BF16 = jnp.bfloat16


def choose_kernel(ins, start, left_ref, vertex_ref, right_ref, l_ref, v_ref, r_ref):
    k = pl.program_id(0)
    sinks = right_ref.shape[1]
    slice_time = ins[k] * (LT // NS)
    source_time = lax.rem(start[0] + lax.axis_index("row"), LT)
    l_ref[0] = left_ref[0, 0] * jnp.where(slice_time < source_time, -1.0, 1.0).astype(F32)
    v_ref[0] = vertex_ref[0]
    for u in range(sinks):
        sink_time = lax.rem(start[1] + lax.axis_index("col") * sinks + u, LT)
        sign = jnp.where(sink_time < slice_time, -1.0, 1.0).astype(F32)
        for part in range(2):
            r_ref[0, part, u] = right_ref[0, u, part] * sign


def choose(left_prop, vertex, right_t, insertions, window_start):
    count = insertions.shape[0]
    _, _, _, lrows, m = left_prop.shape
    vrows = vertex.shape[2]
    sinks, cols = right_t.shape[1], right_t.shape[3]
    return pl.pallas_call(
        choose_kernel,
        grid_spec=pltpu.PrefetchScalarGridSpec(
            num_scalar_prefetch=2,
            grid=(count,),
            in_specs=[
                pl.BlockSpec((1, 1, 2, lrows, m), lambda k, i, *_: (0, i[k], 0, 0, 0)),
                pl.BlockSpec((1, 2, vrows, m), lambda k, i, *_: (i[k], 0, 0, 0)),
                pl.BlockSpec((1, sinks, 2, cols, m), lambda k, i, *_: (i[k], 0, 0, 0, 0)),
            ],
            out_specs=[
                pl.BlockSpec((1, 2, lrows, m), lambda k, *_: (k, 0, 0, 0)),
                pl.BlockSpec((1, 2, vrows, m), lambda k, *_: (k, 0, 0, 0)),
                pl.BlockSpec((1, 2, sinks, cols, m), lambda k, *_: (k, 0, 0, 0, 0)),
            ],
        ),
        out_shape=[
            jax.ShapeDtypeStruct((count, 2, lrows, m), F32),
            jax.ShapeDtypeStruct((count, 2, vrows, m), F32),
            jax.ShapeDtypeStruct((count, 2, sinks, cols, m), F32),
        ],
    )(insertions, window_start, left_prop, vertex, right_t)


def halves(x):
    high = x.astype(BF16)
    return high, (x - high.astype(F32)).astype(BF16)


def dot_nn(a, b):
    return lax.dot_general(a, b, (((1,), (0,)), ((), ())), preferred_element_type=F32)


def dot_nt(a, b):
    return lax.dot_general(a, b, (((1,), (1,)), ((), ())), preferred_element_type=F32)


def main_kernel(
    nz, l_ref, v_ref, r_ref, out_ref,
    v_all, r_all, lv_all, lv_high, lv_low, acc,
    v_send_z, v_send, v_recv, r_send, r_recv, lv_send, lv_recv,
):
    count, _, lrows, m = l_ref.shape
    vrows = v_ref.shape[2]
    sinks = out_ref.shape[1]
    rrows = r_ref.shape[1]
    half = rrows // 2
    cols = half // sinks
    ncol = 4
    row, c = lax.axis_index("row"), lax.axis_index("col")
    z, h = row // 2, lax.rem(row, 2)
    cx = c + 1 - 2 * lax.rem(c, 2)
    cy = lax.rem(c + 2, ncol)
    cd = lax.rem(cx + 2, ncol)
    sib = (2 * z + 1 - h, c)
    to_x, to_y = (row, cx), (row, cy)
    up, down = (row + 2, c), (row - 2, c)

    barrier = pltpu.get_barrier_semaphore()
    for dz in range(1, nz):
        pl.semaphore_signal(barrier, inc=1, device_id=(2 * lax.rem(z + dz, nz) + h, c), device_id_type=MESH)
    for dev in (sib, to_x, to_y):
        pl.semaphore_signal(barrier, inc=1, device_id=dev, device_id_type=MESH)
    pl.semaphore_wait(barrier, nz - 1 + 3)

    pending = []

    def send(src, dst, ssem, rsem, dev, when=None):
        def make():
            return pltpu.make_async_remote_copy(
                src_ref=src(), dst_ref=dst(), send_sem=ssem(), recv_sem=rsem(), device_id=dev, device_id_type=MESH
            )

        if when is None:
            make().start()
        else:
            pl.when(when)(lambda: make().start())
        pending.append((when, make))

    def arrived(dst, rsem):
        pltpu.make_async_remote_copy(
            src_ref=dst, dst_ref=dst, send_sem=v_send_z.at[0], recv_sem=rsem, device_id=sib, device_id_type=MESH
        ).wait_recv()

    def v_slot(zs, hs, cs):
        return v_all.at[:, :, pl.ds(pl.multiple_of(((2 * zs + hs) * ncol + cs) * vrows, vrows), vrows), :]

    def v_sem(zs, hs, cs):
        return v_recv.at[(2 * zs + hs) * ncol + cs]

    for dz in range(1, nz):
        send(
            lambda: v_ref, lambda: v_slot(z, h, c), lambda dz=dz: v_send_z.at[dz], lambda: v_sem(z, h, c),
            (2 * lax.rem(z + dz, nz) + h, c),
        )

    def r_pass(kind, zs, k, src, dev, when=None):
        send(
            src, lambda: r_all.at[2 * zs + h, k], lambda: r_send.at[kind, zs, k], lambda: r_recv.at[2 * zs + h, k],
            dev, when,
        )

    has_up, has_down = z < nz - 1, z > 0

    def r_own(k):
        r_pass(0, z, k, lambda: r_ref.at[k], up, has_up)
        r_pass(1, z, k, lambda: r_ref.at[k], down, has_down)

    r_own(0)

    def v_pass(kind, j, mm, src, zs, cs, dev):
        send(src, lambda: v_slot(zs, h, cs), lambda: v_send.at[kind, j, mm], lambda: v_sem(zs, h, cs), dev)

    for mm in range(nz):
        zs = lax.rem(z + mm, nz)
        if mm == 0:
            src = lambda: v_ref
        else:
            src = lambda zs=zs: v_slot(zs, h, c)
            arrived(v_slot(zs, h, c), v_sem(zs, h, c))
        v_pass(0, 0, mm, src, zs, c, to_x)
        v_pass(1, 0, mm, src, zs, c, to_y)
        v_pass(2, 0, mm, src, zs, c, sib)
    v_all[:, :, pl.ds(pl.multiple_of((row * ncol + c) * vrows, vrows), vrows), :] = v_ref[...]

    for k in range(1, count):
        r_own(k)
    for k in range(count):
        r_pass(2, z, k, lambda k=k: r_ref.at[k], sib)
    r_all[row] = r_ref[...]

    hops = {}
    for d in range(1, nz):
        low_ok, high_ok = z - d >= 0, z + d < nz
        hops[d] = (
            (0, up, z - d, low_ok, jnp.logical_and(low_ok, has_up)),
            (1, down, z + d, high_ok, jnp.logical_and(high_ok, has_down)),
        )

    def r_step(d, pieces=range(count)):
        for k in pieces:
            for kind, toward, zs, ok, onward in hops[d]:
                src = lambda zs=zs, k=k: r_all.at[2 * zs + h, k]

                @pl.when(ok)
                def _(zs=zs, k=k, src=src):
                    arrived(src(), r_recv.at[2 * zs + h, k])

                if d < nz - 1:
                    r_pass(kind, zs, k, src, toward, onward)
                r_pass(2, zs, k, src, sib, ok)

    for mm in range(nz):
        zs = lax.rem(z + mm, nz)
        arrived(v_slot(zs, h, cx), v_sem(zs, h, cx))
        src = lambda zs=zs: v_slot(zs, h, cx)
        if mm < nz // 2:
            v_pass(1, 1, mm, src, zs, cx, to_y)
        v_pass(2, 1, mm, src, zs, cx, sib)
        arrived(v_slot(zs, h, cy), v_sem(zs, h, cy))
        src = lambda zs=zs: v_slot(zs, h, cy)
        if mm >= nz // 2:
            v_pass(0, 1, mm, src, zs, cy, to_x)
        v_pass(2, 2, mm, src, zs, cy, sib)
    for mm in range(nz):
        zs = lax.rem(z + mm, nz)
        arrived(v_slot(zs, h, cd), v_sem(zs, h, cd))
        v_pass(2, 3, mm, lambda zs=zs: v_slot(zs, h, cd), zs, cd, sib)
    for mm in range(nz):
        zs = lax.rem(z + mm, nz)
        for cs in (c, cx, cy, cd):
            arrived(v_slot(zs, 1 - h, cs), v_sem(zs, 1 - h, cs))

    def lv_piece(cs, k, part):
        return lv_all.at[cs, k, part]

    def lv_pass(kind, fwd, k, part, cs, dev):
        send(
            lambda: lv_piece(cs, k, part), lambda: lv_piece(cs, k, part),
            lambda: lv_send.at[kind, fwd, k, part], lambda: lv_recv.at[cs, k, part], dev,
        )

    def split_lv(cs, k, part):
        high, low = halves(lv_all[cs, k, part])
        at = pl.ds(pl.multiple_of(part * m + cs * lrows, lrows), lrows)
        lv_high[k, at, :] = high
        lv_low[k, at, :] = low

    for k in range(count):
        xh, xl = halves(l_ref[k].reshape(2 * lrows, m))
        prods = []
        for part in range(2):
            vh, vl = halves(v_all[k, part])
            prods.append(dot_nn(xh, vh) + dot_nn(xl, vh) + dot_nn(xh, vl))
        lv_all[c, k, 0] = prods[0][:lrows] - prods[1][lrows:]
        lv_all[c, k, 1] = prods[1][:lrows] + prods[0][lrows:]
        for part in range(2):
            lv_pass(0, 0, k, part, c, to_x)
            lv_pass(1, 0, k, part, c, to_y)

    r_step(1)

    for k in range(count):
        for part in range(2):
            split_lv(c, k, part)
    for k in range(count):
        for part in range(2):
            arrived(lv_piece(cx, k, part), lv_recv.at[cx, k, part])
            if part == 0:
                lv_pass(1, 1, k, part, cx, to_y)
            arrived(lv_piece(cy, k, part), lv_recv.at[cy, k, part])
            if part == 1:
                lv_pass(0, 1, k, part, cy, to_x)
            split_lv(cx, k, part)
            split_lv(cy, k, part)
    for d in range(2, nz - 1):
        r_step(d)
    for k in range(count):
        for part in range(2):
            arrived(lv_piece(cd, k, part), lv_recv.at[cd, k, part])
            split_lv(cd, k, part)

    def chip(i, carry):
        d = (i + 1) // 2
        q = z + d * (1 - 2 * lax.rem(i, 2))

        @pl.when(jnp.logical_and(q >= 0, q < nz))
        def _():
            for k in range(count):
                if nz > 2:
                    pl.when(d == nz - 1)(lambda k=k: r_step(nz - 1, [k]))

                def one(n, carry, k=k):
                    j = h + n * (1 - 2 * h)

                    @pl.when(n == 1)
                    def _():
                        arrived(r_all.at[2 * q + j, k], r_recv.at[2 * q + j, k])

                    yh, yl = halves(r_all[2 * q + j, k])
                    for part in range(2):
                        at = pl.ds(part * m, m)
                        p = (
                            dot_nt(lv_high[k, at, :], yh)
                            + dot_nt(lv_low[k, at, :], yh)
                            + dot_nt(lv_high[k, at, :], yl)
                        )
                        if k == 0:
                            acc[j, at, :] = p
                        else:
                            acc[j, at, :] += p
                    return carry

                lax.fori_loop(0, 2, one, 0)
            real, imag = [], []
            for j in range(2):
                real.append(acc[j, pl.ds(0, m), pl.ds(0, half)] - acc[j, pl.ds(m, m), pl.ds(half, half)])
                imag.append(acc[j, pl.ds(0, m), pl.ds(half, half)] + acc[j, pl.ds(m, m), pl.ds(0, half)])
            lanes = pl.ds(pl.multiple_of(q * 2 * cols, 2 * cols), 2 * cols)
            for u in range(sinks):
                cut = slice(u * cols, (u + 1) * cols)
                out_ref[0, u, 0, :, lanes] = jnp.concatenate([real[0][:, cut], real[1][:, cut]], axis=1)
                out_ref[0, u, 1, :, lanes] = jnp.concatenate([imag[0][:, cut], imag[1][:, cut]], axis=1)

        return carry

    lax.fori_loop(0, 2 * nz - 1, chip, 0)

    for when, make in pending:
        if when is None:
            make().wait_send()
        else:
            pl.when(when)(lambda make=make: make().wait_send())


def exchange_and_contract(nrow, ncol, chosen_left, chosen_vertex, chosen_right):
    count, _, lrows, m = chosen_left.shape
    vrows = chosen_vertex.shape[2]
    sinks, cols = chosen_right.shape[2], chosen_right.shape[3]
    rrows = 2 * sinks * cols
    nz = nrow // 2
    dma = pltpu.SemaphoreType.DMA
    vmem = pl.BlockSpec(memory_space=pltpu.VMEM)
    return pl.pallas_call(
        functools.partial(main_kernel, nz),
        out_shape=jax.ShapeDtypeStruct((1, sinks, 2, m, nrow * cols), F32),
        in_specs=[vmem, vmem, vmem],
        out_specs=vmem,
        scratch_shapes=[
            pltpu.VMEM((count, 2, nrow * ncol * vrows, m), F32),
            pltpu.VMEM((nrow, count, rrows, m), F32),
            pltpu.VMEM((ncol, count, 2, lrows, m), F32),
            pltpu.VMEM((count, 2 * m, m), BF16),
            pltpu.VMEM((count, 2 * m, m), BF16),
            pltpu.VMEM((2, 2 * m, rrows), F32),
            dma((nz,)),
            dma((3, 4, nz)),
            dma((nrow * ncol,)),
            dma((3, nz, count)),
            dma((nrow, count)),
            dma((2, 2, count, 2)),
            dma((ncol, count, 2)),
        ],
        compiler_params=pltpu.CompilerParams(
            collective_id=0, has_side_effects=True, vmem_limit_bytes=48 * 1024 * 1024
        ),
    )(chosen_left, chosen_vertex, chosen_right.reshape(count, rrows, m))


def complex_product(first, second):
    highest = lax.Precision.HIGHEST
    first_re, first_im = first[..., 0, :, :], first[..., 1, :, :]
    second_re, second_im = second[..., 0, :, :], second[..., 1, :, :]
    real_part = jnp.matmul(first_re, second_re, precision=highest) - jnp.matmul(first_im, second_im, precision=highest)
    imag_part = jnp.matmul(first_re, second_im, precision=highest) + jnp.matmul(first_im, second_re, precision=highest)
    return jnp.stack([real_part, imag_part], axis=-3)


def pick(array, insertions, axis):
    parts = [lax.dynamic_index_in_dim(array, insertions[k], axis, keepdims=True) for k in range(insertions.shape[0])]
    return jnp.concatenate(parts, axis=axis)


def general(left_prop, vertex, right_prop, insertions, window_start):
    source_count = left_prop.shape[0]
    sink_count = right_prop.shape[1]
    source_slots = lax.axis_index("row") * source_count + jnp.arange(source_count, dtype=jnp.int32)
    sink_slots = lax.axis_index("col") * sink_count + jnp.arange(sink_count, dtype=jnp.int32)
    slice_times = insertions * (LT // NS)
    source_times = (window_start[0] + source_slots) % LT
    sink_times = (window_start[1] + sink_slots) % LT
    left_sign = jnp.where(slice_times[None, :] < source_times[:, None], -1.0, 1.0).astype(F32)
    right_sign = jnp.where(sink_times[None, :] < slice_times[:, None], -1.0, 1.0).astype(F32)
    chosen_left = pick(left_prop, insertions, 1) * left_sign[:, :, None, None, None]
    chosen_right = pick(right_prop, insertions, 0) * right_sign[:, :, None, None, None]
    vertex_full = lax.all_gather(pick(vertex, insertions, 0), ("row", "col"), axis=2, tiled=True)
    through = complex_product(chosen_left, vertex_full[None])
    through = lax.all_gather(through, "col", axis=3, tiled=True)
    right_full = lax.all_gather(chosen_right, "row", axis=4, tiled=True)
    summed = complex_product(through[:, 0, None], right_full[0][None])
    for k in range(1, insertions.shape[0]):
        summed = summed + complex_product(through[:, k, None], right_full[k][None])
    return summed


def per_device(nrow, ncol, left_prop, vertex, right_prop, insertions, window_start):
    source_count = left_prop.shape[0]
    lrows, m = left_prop.shape[3:]
    fits = (
        source_count == 1 and ncol == 4 and nrow % 2 == 0 and nrow >= 4 and vertex.shape[2] % 8 == 0
        and lrows % 16 == 0 and m % 128 == 0 and 2 * right_prop.shape[4] == 128
        and right_prop.shape[1] * right_prop.shape[4] == 128
    )
    if not fits:
        return general(left_prop, vertex, right_prop, insertions, window_start)
    chosen = choose(left_prop, vertex, jnp.swapaxes(right_prop, 3, 4), insertions, window_start)
    return exchange_and_contract(nrow, ncol, *chosen)


def solution(mesh):
    return jax.shard_map(
        functools.partial(per_device, mesh.shape["row"], mesh.shape["col"]),
        mesh=mesh,
        in_specs=(
            P("row", None, None, "col", None),
            P(None, None, ("row", "col"), None),
            P(None, "col", None, None, "row"),
            P(),
            P(),
        ),
        out_specs=P("row", "col", None, None, None),
        check_vma=False,
    )
```

```python
import functools

import jax
import jax.numpy as jnp
from jax import lax
from jax.experimental import pallas as pl
from jax.experimental.pallas import tpu as pltpu
from jax.sharding import PartitionSpec as P

NS = 8
LT = 256
MESH = pl.DeviceIdType.MESH
F32 = jnp.float32
BF16 = jnp.bfloat16


def choose_kernel(ins, start, left_ref, vertex_ref, right_ref, l_ref, v_ref, r_ref, sems):
    count, sinks, cols = l_ref.shape[0], right_ref.shape[1], right_ref.shape[3]

    def rows(part, u):
        return pl.ds((part * sinks + u) * cols, cols)

    def copies(k):
        yield pltpu.make_async_copy(vertex_ref.at[ins[k]], v_ref.at[k], sems.at[k, 0])
        yield pltpu.make_async_copy(left_ref.at[0, ins[k]], l_ref.at[k], sems.at[k, 1])
        for u in range(sinks):
            for part in range(2):
                yield pltpu.make_async_copy(
                    right_ref.at[ins[k], u, part], r_ref.at[k, rows(part, u)], sems.at[k, 2 + 2 * u + part]
                )

    for k in range(count):
        for copy in copies(k):
            copy.start()
    for k in range(count):
        for copy in copies(k):
            copy.wait()
        slice_time = ins[k] * (LT // NS)
        source_time = lax.rem(start[0] + lax.axis_index("row"), LT)
        l_ref[k] = l_ref[k] * jnp.where(slice_time < source_time, -1.0, 1.0).astype(F32)
        for u in range(sinks):
            sink_time = lax.rem(start[1] + lax.axis_index("col") * sinks + u, LT)
            sign = jnp.where(sink_time < slice_time, -1.0, 1.0).astype(F32)
            for part in range(2):
                r_ref[k, rows(part, u), :] = r_ref[k, rows(part, u), :] * sign


def choose(left_prop, vertex, right_t, insertions, window_start):
    count = insertions.shape[0]
    _, _, _, lrows, m = left_prop.shape
    vrows = vertex.shape[2]
    sinks, cols = right_t.shape[1], right_t.shape[3]
    smem = pl.BlockSpec(memory_space=pltpu.SMEM)
    hbm = pl.BlockSpec(memory_space=pl.ANY)
    return pl.pallas_call(
        choose_kernel,
        in_specs=[smem, smem, hbm, hbm, hbm],
        out_specs=[pl.BlockSpec(memory_space=pltpu.VMEM)] * 3,
        out_shape=[
            pltpu.VMEM((count, 2, lrows, m), F32),
            pltpu.VMEM((count, 2, vrows, m), F32),
            pltpu.VMEM((count, 2 * sinks * cols, m), F32),
        ],
        scratch_shapes=[pltpu.SemaphoreType.DMA((count, 2 + 2 * sinks))],
    )(insertions, window_start, left_prop, vertex, right_t)


def halves(x):
    high = x.astype(BF16)
    return high, (x - high.astype(F32)).astype(BF16)


def dot_nn(a, b):
    return lax.dot_general(a, b, (((1,), (0,)), ((), ())), preferred_element_type=F32)


def dot_nt(a, b):
    return lax.dot_general(a, b, (((1,), (1,)), ((), ())), preferred_element_type=F32)


def main_kernel(
    nz, l_ref, v_ref, r_ref, out_ref,
    v_all, r_all, lv_all, lv_high, lv_low, acc,
    v_send_z, v_send, v_recv, r_send, r_recv, lv_send, lv_recv,
):
    count, _, lrows, m = l_ref.shape
    vrows = v_ref.shape[2]
    sinks = out_ref.shape[1]
    rrows = r_ref.shape[1]
    half = rrows // 2
    cols = half // sinks
    ncol = 4
    row, c = lax.axis_index("row"), lax.axis_index("col")
    z, h = row // 2, lax.rem(row, 2)
    cx = c + 1 - 2 * lax.rem(c, 2)
    cy = lax.rem(c + 2, ncol)
    cd = lax.rem(cx + 2, ncol)
    sib = (2 * z + 1 - h, c)
    to_x, to_y = (row, cx), (row, cy)
    up, down = (row + 2, c), (row - 2, c)

    barrier = pltpu.get_barrier_semaphore()
    for dz in range(1, nz):
        pl.semaphore_signal(barrier, inc=1, device_id=(2 * lax.rem(z + dz, nz) + h, c), device_id_type=MESH)
    for dev in (sib, to_x, to_y):
        pl.semaphore_signal(barrier, inc=1, device_id=dev, device_id_type=MESH)
    pl.semaphore_wait(barrier, nz - 1 + 3)

    pending = []

    def send(src, dst, ssem, rsem, dev, when=None):
        def make():
            return pltpu.make_async_remote_copy(
                src_ref=src(), dst_ref=dst(), send_sem=ssem(), recv_sem=rsem(), device_id=dev, device_id_type=MESH
            )

        if when is None:
            make().start()
        else:
            pl.when(when)(lambda: make().start())
        pending.append((when, make))

    def arrived(dst, rsem):
        pltpu.make_async_remote_copy(
            src_ref=dst, dst_ref=dst, send_sem=v_send_z.at[0], recv_sem=rsem, device_id=sib, device_id_type=MESH
        ).wait_recv()

    def v_slot(zs, hs, cs):
        return v_all.at[:, :, pl.ds(pl.multiple_of(((2 * zs + hs) * ncol + cs) * vrows, vrows), vrows), :]

    def v_sem(zs, hs, cs):
        return v_recv.at[(2 * zs + hs) * ncol + cs]

    for dz in range(1, nz):
        send(
            lambda: v_ref, lambda: v_slot(z, h, c), lambda dz=dz: v_send_z.at[dz], lambda: v_sem(z, h, c),
            (2 * lax.rem(z + dz, nz) + h, c),
        )

    def r_pass(kind, zs, k, src, dev, when=None):
        send(
            src, lambda: r_all.at[2 * zs + h, k], lambda: r_send.at[kind, zs, k], lambda: r_recv.at[2 * zs + h, k],
            dev, when,
        )

    has_up, has_down = z < nz - 1, z > 0

    def r_own(k):
        r_pass(0, z, k, lambda: r_ref.at[k], up, has_up)
        r_pass(1, z, k, lambda: r_ref.at[k], down, has_down)

    r_own(0)

    def v_pass(kind, j, mm, src, zs, cs, dev):
        send(src, lambda: v_slot(zs, h, cs), lambda: v_send.at[kind, j, mm], lambda: v_sem(zs, h, cs), dev)

    for mm in range(nz):
        zs = lax.rem(z + mm, nz)
        if mm == 0:
            src = lambda: v_ref
        else:
            src = lambda zs=zs: v_slot(zs, h, c)
            arrived(v_slot(zs, h, c), v_sem(zs, h, c))
        v_pass(0, 0, mm, src, zs, c, to_x)
        v_pass(1, 0, mm, src, zs, c, to_y)
        v_pass(2, 0, mm, src, zs, c, sib)
    v_all[:, :, pl.ds(pl.multiple_of((row * ncol + c) * vrows, vrows), vrows), :] = v_ref[...]

    for k in range(1, count):
        r_own(k)
    for k in range(count):
        r_pass(2, z, k, lambda k=k: r_ref.at[k], sib)
    r_all[row] = r_ref[...]

    hops = {}
    for d in range(1, nz):
        low_ok, high_ok = z - d >= 0, z + d < nz
        hops[d] = (
            (0, up, z - d, low_ok, jnp.logical_and(low_ok, has_up)),
            (1, down, z + d, high_ok, jnp.logical_and(high_ok, has_down)),
        )

    def r_step(d, pieces=range(count)):
        for k in pieces:
            for kind, toward, zs, ok, onward in hops[d]:
                src = lambda zs=zs, k=k: r_all.at[2 * zs + h, k]

                @pl.when(ok)
                def _(zs=zs, k=k, src=src):
                    arrived(src(), r_recv.at[2 * zs + h, k])

                if d < nz - 1:
                    r_pass(kind, zs, k, src, toward, onward)
                r_pass(2, zs, k, src, sib, ok)

    for mm in range(nz):
        zs = lax.rem(z + mm, nz)
        arrived(v_slot(zs, h, cx), v_sem(zs, h, cx))
        src = lambda zs=zs: v_slot(zs, h, cx)
        if mm < nz // 2:
            v_pass(1, 1, mm, src, zs, cx, to_y)
        v_pass(2, 1, mm, src, zs, cx, sib)
        arrived(v_slot(zs, h, cy), v_sem(zs, h, cy))
        src = lambda zs=zs: v_slot(zs, h, cy)
        if mm >= nz // 2:
            v_pass(0, 1, mm, src, zs, cy, to_x)
        v_pass(2, 2, mm, src, zs, cy, sib)
    for mm in range(nz):
        zs = lax.rem(z + mm, nz)
        arrived(v_slot(zs, h, cd), v_sem(zs, h, cd))
        v_pass(2, 3, mm, lambda zs=zs: v_slot(zs, h, cd), zs, cd, sib)
    for mm in range(nz):
        zs = lax.rem(z + mm, nz)
        for cs in (c, cx, cy, cd):
            arrived(v_slot(zs, 1 - h, cs), v_sem(zs, 1 - h, cs))

    def lv_piece(cs, k, part):
        return lv_all.at[cs, k, part]

    def lv_pass(kind, fwd, k, part, cs, dev):
        send(
            lambda: lv_piece(cs, k, part), lambda: lv_piece(cs, k, part),
            lambda: lv_send.at[kind, fwd, k, part], lambda: lv_recv.at[cs, k, part], dev,
        )

    def split_lv(cs, k, part):
        high, low = halves(lv_all[cs, k, part])
        at = pl.ds(pl.multiple_of((2 * cs + part) * lrows, lrows), lrows)
        lv_high[k, at, :] = high
        lv_low[k, at, :] = low

    for k in range(count):
        xh, xl = halves(l_ref[k].reshape(2 * lrows, m))
        prods = []
        for part in range(2):
            vh, vl = halves(v_all[k, part])
            prods.append(dot_nn(xh, vh) + dot_nn(xl, vh) + dot_nn(xh, vl))
        lv_all[c, k, 0] = prods[0][:lrows] - prods[1][lrows:]
        lv_all[c, k, 1] = prods[1][:lrows] + prods[0][lrows:]
        for part in range(2):
            lv_pass(0, 0, k, part, c, to_x)
            lv_pass(1, 0, k, part, c, to_y)

    def sibling_step(d):
        for zs, ok in ((z, None),) if d == 0 else tuple((hop[2], hop[3]) for hop in hops[d]):
            for k in range(count):
                src = lambda zs=zs, k=k: (r_all.at[2 * zs + 1 - h, k], r_recv.at[2 * zs + 1 - h, k])
                if ok is None:
                    arrived(*src())
                else:
                    pl.when(ok)(lambda src=src: arrived(*src()))

    def store(q, cs, product):
        at = pl.ds(pl.multiple_of(cs * lrows, lrows), lrows)
        lanes = pl.ds(pl.multiple_of(q * 2 * cols, 2 * cols), 2 * cols)
        real = [p[:lrows, :half] - p[lrows:, half:] for p in product]
        imag = [p[:lrows, half:] + p[lrows:, :half] for p in product]
        for u in range(sinks):
            cut = slice(u * cols, (u + 1) * cols)
            out_ref[0, u, 0, at, lanes] = jnp.concatenate([real[0][:, cut], real[1][:, cut]], axis=1)
            out_ref[0, u, 1, at, lanes] = jnp.concatenate([imag[0][:, cut], imag[1][:, cut]], axis=1)

    def times(k, at, yh, yl):
        high = lv_high[k, at, :]
        return dot_nt(high, yh) + dot_nt(lv_low[k, at, :], yh) + dot_nt(high, yl)

    def contract(sources, first, last):
        def chip(i, carry):
            q = z + (i + 1) // 2 * (1 - 2 * lax.rem(i, 2))

            @pl.when(jnp.logical_and(q >= 0, q < nz))
            def _():
                for j in range(2):
                    for k in range(count):
                        yh, yl = halves(r_all[2 * q + j, k])
                        for cs in sources:
                            at = pl.ds(pl.multiple_of(cs * 2 * lrows, 2 * lrows), 2 * lrows)
                            if k == 0:
                                acc[j, at, :] = times(k, at, yh, yl)
                            else:
                                acc[j, at, :] += times(k, at, yh, yl)
                for cs in sources:
                    at = pl.ds(pl.multiple_of(cs * 2 * lrows, 2 * lrows), 2 * lrows)
                    store(q, cs, [acc[0, at, :], acc[1, at, :]])

            return carry

        lax.fori_loop(first, last, chip, 0)

    for k in range(count):
        for part in range(2):
            split_lv(c, k, part)
    r_step(1)
    sibling_step(0)
    contract([c], 0, 1)
    sibling_step(1)
    contract([c], 1, 3)
    for k in range(count):
        for part in range(2):
            arrived(lv_piece(cx, k, part), lv_recv.at[cx, k, part])
            if part == 0:
                lv_pass(1, 1, k, part, cx, to_y)
            arrived(lv_piece(cy, k, part), lv_recv.at[cy, k, part])
            if part == 1:
                lv_pass(0, 1, k, part, cy, to_x)
            split_lv(cx, k, part)
            split_lv(cy, k, part)
    for d in range(2, nz - 1):
        r_step(d)
    contract([cx, cy], 0, 3)
    for d in range(2, nz - 1):
        sibling_step(d)
    contract([c, cx, cy], 3, 2 * nz - 3)
    for k in range(count):
        for part in range(2):
            arrived(lv_piece(cd, k, part), lv_recv.at[cd, k, part])
            split_lv(cd, k, part)
    contract([cd], 0, 2 * nz - 3)

    def farthest(i, carry):
        q = z + (nz - 1) * (1 - 2 * i)

        @pl.when(jnp.logical_and(q >= 0, q < nz))
        def _():
            for k in range(count):
                r_step(nz - 1, [k])

                def one(n, carry, k=k):
                    j = h + n * (1 - 2 * h)

                    @pl.when(n == 1)
                    def _():
                        arrived(r_all.at[2 * q + j, k], r_recv.at[2 * q + j, k])

                    yh, yl = halves(r_all[2 * q + j, k])
                    for cs in range(0, ncol, 2):
                        at = pl.ds(cs * 2 * lrows, 4 * lrows)
                        if k == 0:
                            acc[j, at, :] = times(k, at, yh, yl)
                        else:
                            acc[j, at, :] += times(k, at, yh, yl)
                    return carry

                lax.fori_loop(0, 2, one, 0)
            for cs in range(ncol):
                at = pl.ds(cs * 2 * lrows, 2 * lrows)
                store(q, cs, [acc[0, at, :], acc[1, at, :]])

        return carry

    lax.fori_loop(0, 2, farthest, 0)

    for when, make in pending:
        if when is None:
            make().wait_send()
        else:
            pl.when(when)(lambda make=make: make().wait_send())


def exchange_and_contract(nrow, ncol, sinks, chosen_left, chosen_vertex, chosen_right):
    count, _, lrows, m = chosen_left.shape
    vrows = chosen_vertex.shape[2]
    rrows = chosen_right.shape[1]
    cols = rrows // (2 * sinks)
    nz = nrow // 2
    dma = pltpu.SemaphoreType.DMA
    vmem = pl.BlockSpec(memory_space=pltpu.VMEM)
    return pl.pallas_call(
        functools.partial(main_kernel, nz),
        out_shape=pltpu.VMEM((1, sinks, 2, m, nrow * cols), F32),
        in_specs=[vmem, vmem, vmem],
        out_specs=vmem,
        scratch_shapes=[
            pltpu.VMEM((count, 2, nrow * ncol * vrows, m), F32),
            pltpu.VMEM((nrow, count, rrows, m), F32),
            pltpu.VMEM((ncol, count, 2, lrows, m), F32),
            pltpu.VMEM((count, 2 * m, m), BF16),
            pltpu.VMEM((count, 2 * m, m), BF16),
            pltpu.VMEM((2, 2 * m, rrows), F32),
            dma((nz,)),
            dma((3, 4, nz)),
            dma((nrow * ncol,)),
            dma((3, nz, count)),
            dma((nrow, count)),
            dma((2, 2, count, 2)),
            dma((ncol, count, 2)),
        ],
        compiler_params=pltpu.CompilerParams(
            collective_id=0, has_side_effects=True, vmem_limit_bytes=42 * 1024 * 1024
        ),
    )(chosen_left, chosen_vertex, chosen_right)


def complex_product(first, second):
    highest = lax.Precision.HIGHEST
    first_re, first_im = first[..., 0, :, :], first[..., 1, :, :]
    second_re, second_im = second[..., 0, :, :], second[..., 1, :, :]
    real_part = jnp.matmul(first_re, second_re, precision=highest) - jnp.matmul(first_im, second_im, precision=highest)
    imag_part = jnp.matmul(first_re, second_im, precision=highest) + jnp.matmul(first_im, second_re, precision=highest)
    return jnp.stack([real_part, imag_part], axis=-3)


def pick(array, insertions, axis):
    parts = [lax.dynamic_index_in_dim(array, insertions[k], axis, keepdims=True) for k in range(insertions.shape[0])]
    return jnp.concatenate(parts, axis=axis)


def general(left_prop, vertex, right_prop, insertions, window_start):
    source_count = left_prop.shape[0]
    sink_count = right_prop.shape[1]
    source_slots = lax.axis_index("row") * source_count + jnp.arange(source_count, dtype=jnp.int32)
    sink_slots = lax.axis_index("col") * sink_count + jnp.arange(sink_count, dtype=jnp.int32)
    slice_times = insertions * (LT // NS)
    source_times = (window_start[0] + source_slots) % LT
    sink_times = (window_start[1] + sink_slots) % LT
    left_sign = jnp.where(slice_times[None, :] < source_times[:, None], -1.0, 1.0).astype(F32)
    right_sign = jnp.where(sink_times[None, :] < slice_times[:, None], -1.0, 1.0).astype(F32)
    chosen_left = pick(left_prop, insertions, 1) * left_sign[:, :, None, None, None]
    chosen_right = pick(right_prop, insertions, 0) * right_sign[:, :, None, None, None]
    vertex_full = lax.all_gather(pick(vertex, insertions, 0), ("row", "col"), axis=2, tiled=True)
    through = complex_product(chosen_left, vertex_full[None])
    through = lax.all_gather(through, "col", axis=3, tiled=True)
    right_full = lax.all_gather(chosen_right, "row", axis=4, tiled=True)
    summed = complex_product(through[:, 0, None], right_full[0][None])
    for k in range(1, insertions.shape[0]):
        summed = summed + complex_product(through[:, k, None], right_full[k][None])
    return summed


def per_device(nrow, ncol, left_prop, vertex, right_prop, insertions, window_start):
    source_count = left_prop.shape[0]
    lrows, m = left_prop.shape[3:]
    fits = (
        source_count == 1 and ncol == 4 and nrow % 2 == 0 and nrow >= 6 and vertex.shape[2] % 8 == 0
        and lrows % 16 == 0 and m % 128 == 0 and 2 * right_prop.shape[4] == 128
        and right_prop.shape[1] * right_prop.shape[4] == 128
    )
    if not fits:
        return general(left_prop, vertex, right_prop, insertions, window_start)
    chosen = choose(left_prop, vertex, jnp.swapaxes(right_prop, 3, 4), insertions, window_start)
    return exchange_and_contract(nrow, ncol, right_prop.shape[1], *chosen)


def solution(mesh):
    return jax.shard_map(
        functools.partial(per_device, mesh.shape["row"], mesh.shape["col"]),
        mesh=mesh,
        in_specs=(
            P("row", None, None, "col", None),
            P(None, None, ("row", "col"), None),
            P(None, "col", None, None, "row"),
            P(),
            P(),
        ),
        out_specs=P("row", "col", None, None, None),
        check_vma=False,
    )
```
